32 devices in a mesh: section: 2 (over y), seq: 4 (over z), chan: 4 (over x, core).
Axes of the slice: x: 2, y: 2, z: 4, core: 2. Of those that a mesh axis runs over, the one named last changes fastest.
Arguments:
- layer_rows: bfloat16 [2, 4096, 8192], P('section', 'seq', 'chan'), may hold values from -6 to 6
- in_weight: bfloat16 [2, 8192, 768], P('section', 'chan'), may hold values from -0.0625 to 0.0625
- long_filter: float32 [2, 4096, 256], P('section', ('seq', 'chan')), may hold values from -2 to 2, as said below
- skip_gain: float32 [2, 256], P('section'), may hold values from -4 to 4
Outputs:
- gated_out: bfloat16 [2, 4096, 256], P('section', ('seq', 'chan'))
The draws below stay inside these ranges and needn't reach their ends.
Inputs may be any that keep to these rules, and one draw needn't show every extreme that they name: `long_filter`: filter taps of each channel.
All inputs are finite; a program needn't handle non-finite values.
Results may differ from the reference program's by a relative error of at most 0.0064.
Values may be sent and summed in bfloat16 or wider, within the bound.
A program may use at most 64 MiB of HBM per device.

```python
import math
import jax
import jax.numpy as jnp

D = 8192
C = 256
SEQ_LEN = 4096
N_SECTION = 2


def draw_long_filter(key, part):
    noise_key, rate_key = jax.random.split(key)
    positions = jnp.arange(SEQ_LEN, dtype=jnp.float32)[None, :, None]
    noise_values = jnp.clip(jax.random.normal(noise_key, (N_SECTION, SEQ_LEN, C), jnp.float32), -6.0, 6.0)
    rate_floor = math.log(0.25 / SEQ_LEN)
    rate_ceiling = math.log(1.0 / 30.0)
    rates = jnp.exp(jax.random.uniform(rate_key, (N_SECTION, 1, C), jnp.float32, rate_floor, rate_ceiling))
    return noise_values * jnp.sqrt(2.0 * rates) * jnp.exp(-rates * positions)


def level_of(key, dims, cuts, least, high):
    loudness, own = 1.0, jax.random.fold_in(key, 6)
    for position, blocks in cuts:
        steps = jnp.exp(jax.random.uniform(jax.random.fold_in(own, position), (blocks,), jnp.float32, least / len(cuts), high / len(cuts)))
        loudness = loudness * jnp.repeat(steps, dims[position] // blocks).reshape([-1 if axis == position else 1 for axis in range(len(dims))])
    return loudness


def bell_draw(own_key, extent, spread, bound, shards=(), kind=jnp.bfloat16):
    result = jax.random.normal(own_key, extent, jnp.float32) * spread
    if len(shards) > 0:
        result = level_of(own_key, extent, shards, -0.22, 0.18) * result
    return jnp.clip(result, min=-bound, max=bound).astype(kind)


def setup_inputs(seed: int = 0) -> dict:
    splits = jax.random.split(jax.random.key(seed), 5)
    return {
        "layer_rows": bell_draw(splits[0], (N_SECTION, SEQ_LEN, D), 1.0, 6.0, ((0, 2), (1, 4), (2, 4))),
        "in_weight": bell_draw(splits[1], (N_SECTION, D, 3 * C), D ** -0.5, 0.0625, ((0, 2), (1, 4))),
        "long_filter": draw_long_filter(jax.random.fold_in(splits[4], 71), 0),
        "skip_gain": bell_draw(splits[3], (N_SECTION, C), 1.0, 4.0, ((0, 2),), jnp.float32),
    }


def reference(layer_rows, in_weight, long_filter, skip_gain):
    results = []
    for section_index in range(N_SECTION):
        source = layer_rows[(section_index - 1) % N_SECTION]
        mixed = jnp.dot(source, in_weight[section_index], preferred_element_type=jnp.float32).astype(jnp.bfloat16)
        queries = mixed[:, :C].astype(jnp.float32)
        keys = mixed[:, C:2 * C].astype(jnp.float32)
        values_part = mixed[:, 2 * C:].astype(jnp.float32)
        signal = keys * values_part
        spectrum = jnp.fft.rfft(signal, n=2 * SEQ_LEN, axis=0) * jnp.fft.rfft(long_filter[section_index], n=2 * SEQ_LEN, axis=0)
        conv = jnp.fft.irfft(spectrum, n=2 * SEQ_LEN, axis=0)[:SEQ_LEN]
        gated = queries * (conv + skip_gain[section_index][None, :] * signal)
        results.append(gated.astype(jnp.bfloat16))
    return jnp.stack(results)
```

```python
import functools
import math

import jax
import jax.numpy as jnp
import numpy as np
from jax import lax
from jax.experimental import pallas as pl
from jax.experimental.pallas import tpu as pltpu
from jax.sharding import PartitionSpec as P

LANES = 128
PIECES = 2
MESH = pl.DeviceIdType.MESH
F32 = jnp.float32


def tables(positions):
    length = 2 * positions
    n1 = positions // LANES
    full = 2 * n1
    kept = n1 + 1
    rows = -(-kept // 8) * 8
    k1 = np.arange(kept)
    angle = 2 * math.pi * ((k1[:, None] * np.arange(n1)[None, :]) % full) / full
    first = np.zeros((2 * rows, n1), np.float32)
    first[:kept] = np.cos(angle)
    first[rows : rows + kept] = -np.sin(angle)
    weight = np.where((k1 == 0) | (k1 == n1), 1.0, 2.0) / length
    last = np.zeros((n1, 2 * rows), np.float32)
    last[:, :kept] = (np.cos(angle) * weight[:, None]).T
    last[:, rows : rows + kept] = -(np.sin(angle) * weight[:, None]).T
    n2 = np.arange(LANES)
    turn = 2 * math.pi * ((np.arange(rows)[:, None] * n2[None, :]) % length) / length
    twist = np.stack([np.cos(turn), np.sin(turn)]).astype(np.float32)
    fine = 2 * math.pi * ((n2[:, None] * n2[None, :]) % LANES) / LANES
    cos, sin = np.cos(fine), np.sin(fine)
    forward = np.block([[cos, -sin], [sin, cos]]).astype(np.float32)
    back = np.block([[cos, sin], [-sin, cos]]).astype(np.float32)
    return first, twist, forward, back, last


def exact(a, b):
    return jnp.dot(a, b, precision=lax.Precision.HIGHEST, preferred_element_type=F32)


def kernel(
    sizes,
    rows_hbm, weight_hbm, filter_hbm, first_ref, twist_ref, forward_ref, back_ref, last_ref,
    out_ref,
    rows_v, wbuf, part, held, fil_in, sig_out, sig_in, query, conv_out, conv_in, gate_out, gate_in,
    fil_line, line, spec_in, fil_spec,
    y_send, y_recv, z_send, z_recv, r_send, r_recv, f_send, f_recv,
    a_send, a_recv, b_send, b_recv, o_send, o_recv, local_sem,
):
    n_sec, n_seq, n_chan, group, share, tile_rows, k_rows = sizes
    sec, z, c = lax.axis_index("section"), lax.axis_index("seq"), lax.axis_index("chan")
    ahead = lax.rem(sec + 1, n_sec)
    behind = lax.rem(sec + n_sec - 1, n_sec)
    half = lax.rem(z, 2)
    mate = z + 1 - 2 * half
    c1 = c + 1 - 2 * lax.rem(c, 2)
    c2 = lax.rem(c + 2, 4)
    c3 = 3 - c
    order = (c3, c2, c1, c)

    def place(s, seq, chan):
        return (s, seq, chan)

    rows_copy = pltpu.make_async_copy(rows_hbm, rows_v, local_sem.at[0])
    rows_copy.start()

    barrier = pltpu.get_barrier_semaphore()

    def greet(i, carry):
        pl.semaphore_signal(
            barrier, inc=1, device_id=place(ahead, i // n_chan, i % n_chan), device_id_type=MESH
        )
        return carry

    lax.fori_loop(0, n_seq * n_chan, greet, 0)
    for other in range(n_chan):
        pl.semaphore_signal(barrier, inc=1, device_id=place(behind, z, other), device_id_type=MESH)
    pl.semaphore_signal(barrier, inc=1, device_id=place(sec, z, c1), device_id_type=MESH)
    pl.semaphore_signal(barrier, inc=1, device_id=place(sec, z, c2), device_id_type=MESH)
    for step in range(1, n_seq):
        pl.semaphore_signal(
            barrier, inc=1, device_id=place(sec, lax.rem(z + step, n_seq), c), device_id_type=MESH
        )
    pl.semaphore_wait(barrier, n_seq * n_chan + n_chan + 2 + n_seq - 1)

    def remote(src, dst, send, recv, target):
        return pltpu.make_async_remote_copy(
            src_ref=src, dst_ref=dst, send_sem=send, recv_sem=recv, device_id=target,
            device_id_type=MESH,
        )

    me = z * n_chan + c

    def filter_copy(i):
        seq, chan = i // n_chan, i % n_chan
        return remote(
            filter_hbm.at[chan * n_seq + seq], fil_in.at[me], f_send.at[i], f_recv.at[me],
            place(behind, seq, chan),
        )

    def filter_wait(i):
        return remote(
            filter_hbm.at[0], fil_in.at[i], f_send.at[i], f_recv.at[i], place(behind, z, c)
        )

    def start_filter(i, carry):
        filter_copy(i).start()
        return carry

    def end_filter(i, carry):
        filter_copy(i).wait_send()
        filter_wait(i).wait_recv()
        return carry

    total = 4 * PIECES

    def piece(k, which):
        return order[k // PIECES] * (2 * PIECES) + which * PIECES + k % PIECES

    def over_y(k):
        at = piece(k, half)
        return remote(
            weight_hbm.at[at], wbuf.at[at], y_send.at[k], y_recv.at[k], place(behind, z, c)
        )

    def over_z(k):
        at = piece(k, half)
        return remote(wbuf.at[at], wbuf.at[at], z_send.at[k], z_recv.at[k], place(sec, mate, c))

    def from_z(k):
        at = piece(k, 1 - half)
        return remote(wbuf.at[at], wbuf.at[at], z_send.at[k], z_recv.at[k], place(sec, mate, c))

    positions = rows_v.shape[0]
    columns = 3 * group
    pos_tile = 256

    def multiply(j, slot):
        block = wbuf[pl.ds(order[j] * 2 * PIECES, 2 * PIECES)].reshape(columns, rows_v.shape[1])

        def tile(t, carry):
            at = pl.multiple_of(t * pos_tile, pos_tile)
            part[slot, :, pl.ds(at, pos_tile)] = lax.dot_general(
                block, rows_v[pl.ds(at, pos_tile), :], (((1,), (1,)), ((), ())),
                preferred_element_type=F32,
            )
            return carry

        lax.fori_loop(0, positions // pos_tile, tile, 0)

    to_pair = remote(part.at[0], held.at[0], r_send.at[0], r_recv.at[0], place(sec, z, c1))
    to_cross = remote(part.at[1], held.at[1], r_send.at[1], r_recv.at[1], place(sec, z, c2))
    to_pair_last = remote(part.at[2], held.at[2], r_send.at[2], r_recv.at[2], place(sec, z, c1))

    def spectrum(source, target):
        mixed = exact(first_ref[...], source[...])
        for a in range(share):
            lanes = slice(a * LANES, (a + 1) * LANES)
            real, imag = mixed[:k_rows, lanes], mixed[k_rows:, lanes]
            span = slice(a * k_rows, (a + 1) * k_rows)
            spec_in[span, :LANES] = real * twist_ref[0] + imag * twist_ref[1]
            spec_in[span, LANES:] = imag * twist_ref[0] - real * twist_ref[1]
        target[...] = exact(spec_in[...], forward_ref[...])

    def process(j):
        for k in range(j * PIECES, (j + 1) * PIECES):
            from_z(k).wait_recv()
        multiply(j, j)
        if j == 0:
            to_pair.start()
        if j == 1:
            to_pair.wait_recv()
            part[1] = part[1] + held[0]
            to_cross.start()
        if j == 2:
            to_pair_last.start()

    over_y(0).start()
    over_y(1).start()
    lax.fori_loop(0, n_seq * n_chan, start_filter, 0)
    rows_copy.wait()
    for k in range(total):
        over_y(k).wait_recv()
        over_z(k).start()
        over_y(k).wait_send()
        if k + 2 < total:
            over_y(k + 2).start()
        if k == PIECES:
            lax.fori_loop(0, n_seq * n_chan, end_filter, 0)
            per = fil_in.shape[2] // LANES
            for i in range(n_seq * n_chan):
                for r in range(per):
                    for a in range(share):
                        fil_line[i * per + r : i * per + r + 1, a * LANES : (a + 1) * LANES] = (
                            fil_in[i, a : a + 1, r * LANES : (r + 1) * LANES]
                        )
            spectrum(fil_line, fil_spec)
        if k % PIECES == PIECES - 1 and k >= PIECES:
            process(k // PIECES - 1)
    process(3)
    to_pair_last.wait_recv()
    to_cross.wait_recv()
    mixed = (part[3] + held[2] + held[1]).astype(jnp.bfloat16).astype(F32)
    signal = mixed[group : 2 * group] * mixed[2 * group :]
    for r in range(tile_rows):
        lanes = slice(r * LANES, (r + 1) * LANES)
        sig_out[:, r, :] = signal[:, lanes]
        query[:, r, :] = mixed[:group, lanes]

    def sig_copy(step):
        to = lax.rem(z + step, n_seq)
        return remote(
            sig_out.at[pl.ds(to * share, share)], sig_in.at[z], a_send.at[step], a_recv.at[step],
            place(sec, to, c),
        )

    def sig_wait(step):
        source = lax.rem(z + n_seq - step, n_seq)
        return remote(
            sig_out.at[pl.ds(0, share)], sig_in.at[source], a_send.at[step], a_recv.at[step],
            place(sec, source, c),
        )

    for step in range(1, n_seq):
        sig_copy(step).start()
    sig_in[z] = sig_out[pl.ds(z * share, share)]
    for step in range(1, n_seq):
        sig_wait(step).wait_recv()

    for a in range(share):
        line[:, a * LANES : (a + 1) * LANES] = sig_in[:, a].reshape(n_seq * tile_rows, LANES)
    mixed_first = exact(first_ref[...], line[...])
    for a in range(share):
        lanes = slice(a * LANES, (a + 1) * LANES)
        real, imag = mixed_first[:k_rows, lanes], mixed_first[k_rows:, lanes]
        span = slice(a * k_rows, (a + 1) * k_rows)
        spec_in[span, :LANES] = real * twist_ref[0] + imag * twist_ref[1]
        spec_in[span, LANES:] = imag * twist_ref[0] - real * twist_ref[1]
    spec = exact(spec_in[...], forward_ref[...])
    sr, si = spec[:, :LANES], spec[:, LANES:]
    fr, fi = fil_spec[:, :LANES], fil_spec[:, LANES:]
    spec_in[:, :LANES] = sr * fr - si * fi
    spec_in[:, LANES:] = sr * fi + si * fr
    inner = exact(spec_in[...], back_ref[...])
    turned = []
    for a in range(share):
        span = slice(a * k_rows, (a + 1) * k_rows)
        real, imag = inner[span, :LANES], inner[span, LANES:]
        turned.append(
            jnp.concatenate(
                [
                    real * twist_ref[0] - imag * twist_ref[1],
                    imag * twist_ref[0] + real * twist_ref[1],
                ],
                axis=0,
            )
        )
    conv = exact(last_ref[...], jnp.concatenate(turned, axis=1))
    for a in range(share):
        conv_out[:, a] = conv[:, a * LANES : (a + 1) * LANES].reshape(n_seq, tile_rows, LANES)

    def conv_copy(step):
        to = lax.rem(z + step, n_seq)
        return remote(
            conv_out.at[to], conv_in.at[z], b_send.at[step], b_recv.at[step], place(sec, to, c)
        )

    def conv_wait(step):
        source = lax.rem(z + n_seq - step, n_seq)
        return remote(
            conv_out.at[0], conv_in.at[source], b_send.at[step], b_recv.at[step],
            place(sec, source, c),
        )

    for step in range(1, n_seq):
        conv_copy(step).start()
    conv_in[z] = conv_out[z]
    for step in range(1, n_seq):
        conv_wait(step).wait_recv()

    per = tile_rows // n_chan
    for r in range(tile_rows):
        gated = query[:, r, :] * conv_in[:, :, r, :].reshape(group, LANES)
        gate_out[r // per, :, (r % per) * LANES : (r % per + 1) * LANES] = gated.astype(
            jnp.bfloat16
        )

    def gate_copy(to):
        return remote(
            gate_out.at[to], gate_in.at[c], o_send.at[to], o_recv.at[c], place(ahead, z, to)
        )

    def gate_wait(source):
        return remote(
            gate_out.at[0], gate_in.at[source], o_send.at[source], o_recv.at[source],
            place(ahead, z, source),
        )

    for to in range(n_chan):
        gate_copy(to).start()
    for source in range(n_chan):
        gate_wait(source).wait_recv()
    whole = gate_in[...].astype(F32).reshape(n_chan * group, per * LANES)
    out_ref[...] = whole.T.astype(jnp.bfloat16)

    for k in range(total):
        over_z(k).wait_send()
    to_pair.wait_send()
    to_cross.wait_send()
    to_pair_last.wait_send()
    for step in range(1, n_seq):
        sig_copy(step).wait_send()
        conv_copy(step).wait_send()
    for to in range(n_chan):
        gate_copy(to).wait_send()


def body(n_sec, n_seq, n_chan, layer_rows, in_weight, long_filter, skip_gain):
    chan_width = long_filter.shape[2]
    block = long_filter.shape[1]
    positions, features = layer_rows.shape[1:]
    group = chan_width // n_chan
    share = group // n_seq
    tile_rows = positions // LANES
    n1 = n_seq * tile_rows
    first, twist, forward, back, last = tables(n_seq * positions)
    k_rows = twist.shape[1]
    weight = in_weight[0].reshape(features, 3, n_chan, group).transpose(2, 1, 3, 0)
    width = 3 * group // (2 * PIECES)
    weight = weight.reshape(n_chan * 2 * PIECES, width, features)
    at_start = lax.axis_index(("seq", "chan")) == 0
    tap = jnp.where(at_start, skip_gain[0], 0.0)
    taps = jnp.concatenate([long_filter[0, :1] + tap[None, :], long_filter[0, 1:]], axis=0)
    taps = taps.T.reshape(n_chan * n_seq, share, block)
    sizes = (n_sec, n_seq, n_chan, group, share, tile_rows, k_rows)
    vmem = pl.BlockSpec(memory_space=pltpu.VMEM)
    hbm = pl.BlockSpec(memory_space=pl.ANY)
    dma = pltpu.SemaphoreType.DMA
    devices = n_seq * n_chan
    total = 4 * PIECES
    scratch = [
        pltpu.VMEM((positions, features), jnp.bfloat16),
        pltpu.VMEM(weight.shape, jnp.bfloat16),
        pltpu.VMEM((4, 3 * group, positions), F32),
        pltpu.VMEM((3, 3 * group, positions), F32),
        pltpu.VMEM((devices, share, block), F32),
        pltpu.VMEM((group, tile_rows, LANES), F32),
        pltpu.VMEM((n_seq, share, tile_rows, LANES), F32),
        pltpu.VMEM((group, tile_rows, LANES), F32),
        pltpu.VMEM((n_seq, share, tile_rows, LANES), F32),
        pltpu.VMEM((n_seq, share, tile_rows, LANES), F32),
        pltpu.VMEM((n_chan, group, block), jnp.bfloat16),
        pltpu.VMEM((n_chan, group, block), jnp.bfloat16),
        pltpu.VMEM((n1, share * LANES), F32),
        pltpu.VMEM((n1, share * LANES), F32),
        pltpu.VMEM((share * k_rows, 2 * LANES), F32),
        pltpu.VMEM((share * k_rows, 2 * LANES), F32),
        dma((total,)), dma((total,)), dma((total,)), dma((total,)), dma((3,)), dma((3,)),
        dma((devices,)), dma((devices,)), dma((n_seq,)), dma((n_seq,)), dma((n_seq,)),
        dma((n_seq,)), dma((n_chan,)), dma((n_chan,)), dma((1,)),
    ]
    out = pl.pallas_call(
        functools.partial(kernel, sizes),
        out_shape=jax.ShapeDtypeStruct((block, chan_width), jnp.bfloat16),
        in_specs=[hbm, hbm, hbm, vmem, vmem, vmem, vmem, vmem],
        out_specs=vmem,
        scratch_shapes=scratch,
        compiler_params=pltpu.CompilerParams(
            collective_id=0, has_side_effects=True, vmem_limit_bytes=48 * 2**20
        ),
        cost_estimate=pl.CostEstimate(
            flops=2 * positions * features * 3 * chan_width,
            bytes_accessed=10 * 2**20, transcendentals=0,
        ),
    )(layer_rows[0], weight, taps, first, twist, forward, back, last)
    return out[None]


def solution(mesh):
    in_specs = (
        P("section", "seq", "chan"),
        P("section", "chan", None),
        P("section", ("seq", "chan"), None),
        P("section", None),
    )
    out_specs = P("section", ("seq", "chan"), None)
    call = functools.partial(
        body, mesh.shape["section"], mesh.shape["seq"], mesh.shape["chan"]
    )
    return jax.shard_map(call, mesh=mesh, in_specs=in_specs, out_specs=out_specs, check_vma=False)
```

```python
import functools
import math

import jax
import jax.numpy as jnp
import numpy as np
from jax import lax
from jax.experimental import pallas as pl
from jax.experimental.pallas import tpu as pltpu
from jax.sharding import PartitionSpec as P

LANES = 128
PIECES = 2
BLOCKS = 6
AHEAD = 4
MESH = pl.DeviceIdType.MESH
F32 = jnp.float32


def tables(positions):
    length = 2 * positions
    n1 = positions // LANES
    full = 2 * n1
    kept = n1 + 1
    rows = -(-kept // 8) * 8
    k1 = np.arange(kept)
    angle = 2 * math.pi * ((k1[:, None] * np.arange(n1)[None, :]) % full) / full
    first = np.zeros((2 * rows, n1), np.float32)
    first[:kept] = np.cos(angle)
    first[rows : rows + kept] = -np.sin(angle)
    weight = np.where((k1 == 0) | (k1 == n1), 1.0, 2.0) / length
    last = np.zeros((n1, 2 * rows), np.float32)
    last[:, :kept] = (np.cos(angle) * weight[:, None]).T
    last[:, rows : rows + kept] = -(np.sin(angle) * weight[:, None]).T
    n2 = np.arange(LANES)
    turn = 2 * math.pi * ((np.arange(rows)[:, None] * n2[None, :]) % length) / length
    twist = np.stack([np.cos(turn), np.sin(turn)]).astype(np.float32)
    fine = 2 * math.pi * ((n2[:, None] * n2[None, :]) % LANES) / LANES
    cos, sin = np.cos(fine), np.sin(fine)
    forward = np.block([[cos, -sin], [sin, cos]]).astype(np.float32)
    back = np.block([[cos, sin], [-sin, cos]]).astype(np.float32)
    return first, twist, forward, back, last


def parts_of(a):
    high = a.astype(jnp.bfloat16)
    return high, (a - high.astype(F32)).astype(jnp.bfloat16)


def exact(a, b):
    a_high, a_low = parts_of(a)
    b_high, b_low = parts_of(b)
    dot = functools.partial(jnp.dot, preferred_element_type=F32)
    return dot(a_high, b_high) + (dot(a_high, b_low) + dot(a_low, b_high))


def kernel(
    sizes,
    rows_hbm, weight_hbm, filter_hbm, first_ref, twist_ref, forward_ref, back_ref, last_ref,
    out_ref,
    rows_v, wbuf, part, held, crossed, fil_in, sig_out, sig_in, query, conv_out, conv_in, gate_out, gate_in,
    stack, line, spec_in, fil_spec, sig_spec,
    y_send, y_recv, z_send, z_recv, r_send, r_recv, f_send, f_recv,
    a_send, a_recv, b_send, b_recv, o_send, o_recv, local_sem,
):
    n_sec, n_seq, n_chan, group, share, tile_rows, k_rows = sizes
    sec, z, c = lax.axis_index("section"), lax.axis_index("seq"), lax.axis_index("chan")
    ahead = lax.rem(sec + 1, n_sec)
    behind = lax.rem(sec + n_sec - 1, n_sec)
    half = lax.rem(z, 2)
    mate = z + 1 - 2 * half
    c1 = c + 1 - 2 * lax.rem(c, 2)
    c2 = lax.rem(c + 2, 4)
    own = lax.rem(c, 2)
    other_side, own_side = 1 - c // 2, c // 2

    def place(s, seq, chan):
        return (s, seq, chan)

    rows_copy = pltpu.make_async_copy(rows_hbm, rows_v, local_sem.at[0])
    rows_copy.start()

    barrier = pltpu.get_barrier_semaphore()

    def greet(i, carry):
        pl.semaphore_signal(
            barrier, inc=1, device_id=place(ahead, i // n_chan, i % n_chan), device_id_type=MESH
        )
        return carry

    lax.fori_loop(0, n_seq * n_chan, greet, 0)
    for other in range(n_chan):
        pl.semaphore_signal(barrier, inc=1, device_id=place(behind, z, other), device_id_type=MESH)
    pl.semaphore_signal(barrier, inc=1, device_id=place(sec, z, c1), device_id_type=MESH)
    pl.semaphore_signal(barrier, inc=1, device_id=place(sec, z, c2), device_id_type=MESH)
    for step in range(1, n_seq):
        pl.semaphore_signal(
            barrier, inc=1, device_id=place(sec, lax.rem(z + step, n_seq), c), device_id_type=MESH
        )
    pl.semaphore_wait(barrier, n_seq * n_chan + n_chan + 2 + n_seq - 1)

    def remote(src, dst, send, recv, target):
        return pltpu.make_async_remote_copy(
            src_ref=src, dst_ref=dst, send_sem=send, recv_sem=recv, device_id=target,
            device_id_type=MESH,
        )

    me = z * n_chan + c

    def filter_copy(i):
        seq, chan = i // n_chan, i % n_chan
        return remote(
            filter_hbm.at[chan * n_seq + seq], fil_in.at[me], f_send.at[i], f_recv.at[me],
            place(behind, seq, chan),
        )

    def filter_wait(i):
        return remote(
            filter_hbm.at[0], fil_in.at[i], f_send.at[i], f_recv.at[i], place(behind, z, c)
        )

    def start_filter(i, carry):
        filter_copy(i).start()
        return carry

    def end_filter(i, carry):
        filter_copy(i).wait_send()
        filter_wait(i).wait_recv()
        return carry

    total = BLOCKS * PIECES
    positions, features = rows_v.shape
    depth = features // (2 * PIECES)
    pair = 2 * group

    def block_of(j):
        return (j % 3) * 2 + (other_side if j < 3 else own_side)

    def over_y(k):
        block, at = block_of(k // PIECES), half * PIECES + k % PIECES
        source = weight_hbm.at[
            pl.ds(pl.multiple_of(at * depth, depth), depth),
            pl.ds(pl.multiple_of(block * pair, pair), pair),
        ]
        return remote(
            source, wbuf.at[block, at], y_send.at[k], y_recv.at[k], place(behind, z, c)
        )

    def over_z(k):
        block, at = block_of(k // PIECES), half * PIECES + k % PIECES
        held_piece = wbuf.at[block, at]
        return remote(held_piece, held_piece, z_send.at[k], z_recv.at[k], place(sec, mate, c))

    def from_z(k):
        block, at = block_of(k // PIECES), (1 - half) * PIECES + k % PIECES
        held_piece = wbuf.at[block, at]
        return remote(held_piece, held_piece, z_send.at[k], z_recv.at[k], place(sec, mate, c))

    pos_tile = 256
    own_rows = pl.ds(pl.multiple_of(own * group, group), group)
    pair_rows = pl.ds(pl.multiple_of((1 - own) * group, group), group)

    def multiply(j):
        block = wbuf[block_of(j)].reshape(features, pair).T

        def tile(t, carry):
            at = pl.multiple_of(t * pos_tile, pos_tile)
            part[j, :, pl.ds(at, pos_tile)] = lax.dot_general(
                block, rows_v[pl.ds(at, pos_tile), :], (((1,), (1,)), ((), ())),
                preferred_element_type=F32,
            )
            return carry

        lax.fori_loop(0, positions // pos_tile, tile, 0)

    def to_pair(j):
        return remote(
            part.at[j, pair_rows], held.at[j], r_send.at[j], r_recv.at[j], place(sec, z, c1)
        )

    def to_cross(j):
        return remote(
            part.at[j, own_rows], crossed.at[j], r_send.at[BLOCKS + j], r_recv.at[BLOCKS + j],
            place(sec, z, c2),
        )

    def spectrum(target):
        for a in range(share):
            line[:, a * LANES : (a + 1) * LANES] = stack[a]
        mixed = exact(first_ref[...], line[...])
        for a in range(share):
            lanes = slice(a * LANES, (a + 1) * LANES)
            real, imag = mixed[:k_rows, lanes], mixed[k_rows:, lanes]
            span = slice(a * k_rows, (a + 1) * k_rows)
            spec_in[span, :LANES] = real * twist_ref[0] + imag * twist_ref[1]
            spec_in[span, LANES:] = imag * twist_ref[0] - real * twist_ref[1]
        target[...] = exact(spec_in[...], forward_ref[...])

    def process(j):
        for k in range(j * PIECES, (j + 1) * PIECES):
            from_z(k).wait_recv()
        multiply(j)
        to_pair(j).start()
        if 1 <= j <= 3:
            to_pair(j - 1).wait_recv()
            part[j - 1, own_rows] = part[j - 1, own_rows] + held[j - 1]
            to_cross(j - 1).start()

    lax.fori_loop(0, n_seq * n_chan, start_filter, 0)
    for k in range(AHEAD):
        over_y(k).start()
    rows_copy.wait()
    for k in range(total):
        over_y(k).wait_recv()
        over_z(k).start()
        over_y(k).wait_send()
        if k + AHEAD < total:
            over_y(k + AHEAD).start()
        if k == 2 * PIECES:
            lax.fori_loop(0, n_seq * n_chan, end_filter, 0)
            per = fil_in.shape[2] // LANES
            for i in range(n_seq * n_chan):
                block = fil_in[i].astype(F32)
                for r in range(per):
                    stack[:, i * per + r, :] = block[:, r * LANES : (r + 1) * LANES]
            spectrum(fil_spec)
        if k % PIECES == PIECES - 1 and k >= PIECES:
            process(k // PIECES - 1)
    process(BLOCKS - 1)
    gathered = []
    for t in range(3):
        to_cross(t).wait_recv()
        to_pair(3 + t).wait_recv()
        total_part = part[3 + t, own_rows] + held[3 + t] + crossed[t]
        gathered.append(total_part.astype(jnp.bfloat16).astype(F32))
    query[...] = gathered[0]
    signal = gathered[1] * gathered[2]
    for i in range(n_seq):
        sig_out[i] = signal[i * share : (i + 1) * share].astype(jnp.bfloat16)

    def sig_copy(step):
        to = lax.rem(z + step, n_seq)
        return remote(
            sig_out.at[to], sig_in.at[z], a_send.at[step], a_recv.at[step],
            place(sec, to, c),
        )

    def sig_wait(step):
        source = lax.rem(z + n_seq - step, n_seq)
        return remote(
            sig_out.at[0], sig_in.at[source], a_send.at[step], a_recv.at[step],
            place(sec, source, c),
        )

    for step in range(1, n_seq):
        sig_copy(step).start()
    sig_in[z] = sig_out[z]
    for step in range(1, n_seq):
        sig_wait(step).wait_recv()

    for i in range(n_seq):
        block = sig_in[i].astype(F32)
        for r in range(tile_rows):
            stack[:, i * tile_rows + r, :] = block[:, r * LANES : (r + 1) * LANES]
    spectrum(sig_spec)
    spec = sig_spec[...]
    sr, si = spec[:, :LANES], spec[:, LANES:]
    fr, fi = fil_spec[:, :LANES], fil_spec[:, LANES:]
    spec_in[:, :LANES] = sr * fr - si * fi
    spec_in[:, LANES:] = sr * fi + si * fr
    inner = exact(spec_in[...], back_ref[...])
    turned = []
    for a in range(share):
        span = slice(a * k_rows, (a + 1) * k_rows)
        real, imag = inner[span, :LANES], inner[span, LANES:]
        turned.append(
            jnp.concatenate(
                [
                    real * twist_ref[0] - imag * twist_ref[1],
                    imag * twist_ref[0] + real * twist_ref[1],
                ],
                axis=0,
            )
        )
    conv = exact(last_ref[...], jnp.concatenate(turned, axis=1))
    for a in range(share):
        stack[a] = conv[:, a * LANES : (a + 1) * LANES]
    for i in range(n_seq):
        for r in range(tile_rows):
            conv_out[i, :, r * LANES : (r + 1) * LANES] = stack[:, i * tile_rows + r, :].astype(
                jnp.bfloat16
            )

    def conv_copy(step):
        to = lax.rem(z + step, n_seq)
        return remote(
            conv_out.at[to], conv_in.at[z], b_send.at[step], b_recv.at[step], place(sec, to, c)
        )

    def conv_wait(step):
        source = lax.rem(z + n_seq - step, n_seq)
        return remote(
            conv_out.at[0], conv_in.at[source], b_send.at[step], b_recv.at[step],
            place(sec, source, c),
        )

    for step in range(1, n_seq):
        conv_copy(step).start()
    conv_in[z] = conv_out[z]
    for step in range(1, n_seq):
        conv_wait(step).wait_recv()

    per = tile_rows // n_chan
    gated = query[...] * conv_in[...].astype(F32).reshape(group, positions)
    for to in range(n_chan):
        gate_out[to] = gated[:, to * per * LANES : (to + 1) * per * LANES].astype(jnp.bfloat16)

    def gate_copy(to):
        return remote(
            gate_out.at[to], gate_in.at[c], o_send.at[to], o_recv.at[c], place(ahead, z, to)
        )

    def gate_wait(source):
        return remote(
            gate_out.at[0], gate_in.at[source], o_send.at[source], o_recv.at[source],
            place(ahead, z, source),
        )

    for to in range(n_chan):
        gate_copy(to).start()
    for source in range(n_chan):
        gate_wait(source).wait_recv()
    whole = gate_in[...].astype(F32).reshape(n_chan * group, per * LANES)
    out_ref[...] = whole.T.astype(jnp.bfloat16)

    for k in range(total):
        over_z(k).wait_send()
    for j in range(BLOCKS):
        to_pair(j).wait_send()
    for j in range(3):
        to_cross(j).wait_send()
    for step in range(1, n_seq):
        sig_copy(step).wait_send()
        conv_copy(step).wait_send()
    for to in range(n_chan):
        gate_copy(to).wait_send()


def body(n_sec, n_seq, n_chan, layer_rows, in_weight, long_filter, skip_gain):
    chan_width = long_filter.shape[2]
    block = long_filter.shape[1]
    positions, features = layer_rows.shape[1:]
    group = chan_width // n_chan
    share = group // n_seq
    tile_rows = positions // LANES
    n1 = n_seq * tile_rows
    first, twist, forward, back, last = tables(n_seq * positions)
    k_rows = twist.shape[1]
    weight = in_weight[0]
    pair = 2 * group
    at_start = lax.axis_index(("seq", "chan")) == 0
    tap = jnp.where(at_start, skip_gain[0], 0.0)
    taps = jnp.concatenate([long_filter[0, :1] + tap[None, :], long_filter[0, 1:]], axis=0)
    taps = taps.astype(jnp.bfloat16).T.reshape(n_chan * n_seq, share, block)
    sizes = (n_sec, n_seq, n_chan, group, share, tile_rows, k_rows)
    vmem = pl.BlockSpec(memory_space=pltpu.VMEM)
    hbm = pl.BlockSpec(memory_space=pl.ANY)
    dma = pltpu.SemaphoreType.DMA
    devices = n_seq * n_chan
    total = BLOCKS * PIECES
    scratch = [
        pltpu.VMEM((positions, features), jnp.bfloat16),
        pltpu.VMEM((BLOCKS, 2 * PIECES, features // (2 * PIECES), pair), jnp.bfloat16),
        pltpu.VMEM((BLOCKS, pair, positions), F32),
        pltpu.VMEM((BLOCKS, group, positions), F32),
        pltpu.VMEM((3, group, positions), F32),
        pltpu.VMEM((devices, share, block), jnp.bfloat16),
        pltpu.VMEM((n_seq, share, positions), jnp.bfloat16),
        pltpu.VMEM((n_seq, share, positions), jnp.bfloat16),
        pltpu.VMEM((group, positions), F32),
        pltpu.VMEM((n_seq, share, positions), jnp.bfloat16),
        pltpu.VMEM((n_seq, share, positions), jnp.bfloat16),
        pltpu.VMEM((n_chan, group, block), jnp.bfloat16),
        pltpu.VMEM((n_chan, group, block), jnp.bfloat16),
        pltpu.VMEM((share, n1, LANES), F32),
        pltpu.VMEM((n1, share * LANES), F32),
        pltpu.VMEM((share * k_rows, 2 * LANES), F32),
        pltpu.VMEM((share * k_rows, 2 * LANES), F32),
        pltpu.VMEM((share * k_rows, 2 * LANES), F32),
        dma((total,)), dma((total,)), dma((total,)), dma((total,)), dma((BLOCKS + 3,)),
        dma((BLOCKS + 3,)),
        dma((devices,)), dma((devices,)), dma((n_seq,)), dma((n_seq,)), dma((n_seq,)),
        dma((n_seq,)), dma((n_chan,)), dma((n_chan,)), dma((1,)),
    ]
    out = pl.pallas_call(
        functools.partial(kernel, sizes),
        out_shape=jax.ShapeDtypeStruct((block, chan_width), jnp.bfloat16),
        in_specs=[hbm, hbm, hbm, vmem, vmem, vmem, vmem, vmem],
        out_specs=vmem,
        scratch_shapes=scratch,
        compiler_params=pltpu.CompilerParams(
            collective_id=0, has_side_effects=True, vmem_limit_bytes=48 * 2**20
        ),
        cost_estimate=pl.CostEstimate(
            flops=2 * positions * features * 3 * chan_width,
            bytes_accessed=10 * 2**20, transcendentals=0,
        ),
    )(layer_rows[0], weight, taps, first, twist, forward, back, last)
    return out[None]


def solution(mesh):
    in_specs = (
        P("section", "seq", "chan"),
        P("section", "chan", None),
        P("section", ("seq", "chan"), None),
        P("section", None),
    )
    out_specs = P("section", ("seq", "chan"), None)
    call = functools.partial(
        body, mesh.shape["section"], mesh.shape["seq"], mesh.shape["chan"]
    )
    return jax.shard_map(call, mesh=mesh, in_specs=in_specs, out_specs=out_specs, check_vma=False)
```

```python
import functools
import math

import jax
import jax.numpy as jnp
import numpy as np
from jax import lax
from jax.experimental import pallas as pl
from jax.experimental.pallas import tpu as pltpu
from jax.sharding import PartitionSpec as P

LANES = 128
PIECES = 2
BLOCKS = 6
AHEAD = 4
MESH = pl.DeviceIdType.MESH
F32 = jnp.float32


def tables(positions):
    length = 2 * positions
    n1 = positions // LANES
    full = 2 * n1
    kept = n1 + 1
    rows = -(-kept // 8) * 8
    k1 = np.arange(kept)
    angle = 2 * math.pi * ((k1[:, None] * np.arange(n1)[None, :]) % full) / full
    first = np.zeros((2 * rows, n1), np.float32)
    first[:kept] = np.cos(angle)
    first[rows : rows + kept] = -np.sin(angle)
    weight = np.where((k1 == 0) | (k1 == n1), 1.0, 2.0) / length
    last = np.zeros((n1, 2 * rows), np.float32)
    last[:, :kept] = (np.cos(angle) * weight[:, None]).T
    last[:, rows : rows + kept] = -(np.sin(angle) * weight[:, None]).T
    n2 = np.arange(LANES)
    turn = 2 * math.pi * ((np.arange(rows)[:, None] * n2[None, :]) % length) / length
    twist = np.stack([np.cos(turn), np.sin(turn)]).astype(np.float32)
    fine = 2 * math.pi * ((n2[:, None] * n2[None, :]) % LANES) / LANES
    cos, sin = np.cos(fine), np.sin(fine)
    forward = np.block([[cos, -sin], [sin, cos]]).astype(np.float32)
    back = np.block([[cos, sin], [-sin, cos]]).astype(np.float32)
    return first, twist, forward, back, last


def packed_tables(positions):
    first, twist, forward, back, last = tables(positions)
    wide = [forward, back, np.concatenate([twist[0], twist[1]], axis=1), first, last]
    return np.concatenate([np.pad(t, ((0, 0), (0, 2 * LANES - t.shape[1]))) for t in wide])


def parts_of(a):
    high = a.astype(jnp.bfloat16)
    return high, (a - high.astype(F32)).astype(jnp.bfloat16)


def exact(a, b):
    a_high, a_low = parts_of(a)
    b_high, b_low = parts_of(b)
    dot = functools.partial(jnp.dot, preferred_element_type=F32)
    return dot(a_high, b_high) + (dot(a_high, b_low) + dot(a_low, b_high))


def kernel(
    sizes,
    rows_hbm, weight_hbm, filter_hbm, table_hbm,
    out_ref,
    table, rows_v, wbuf, part, held, crossed, fil_in, sig_out, sig_in, query, conv_out, conv_in, gate_out, gate_in,
    stack, line, spec_in, fil_spec, sig_spec,
    y_send, y_recv, z_send, z_recv, r_send, r_recv, f_send, f_recv,
    a_send, a_recv, b_send, b_recv, o_send, o_recv, local_sem,
):
    n_sec, n_seq, n_chan, group, share, tile_rows, k_rows = sizes
    sec, z, c = lax.axis_index("section"), lax.axis_index("seq"), lax.axis_index("chan")
    ahead = lax.rem(sec + 1, n_sec)
    behind = lax.rem(sec + n_sec - 1, n_sec)
    half = lax.rem(z, 2)
    mate = z + 1 - 2 * half
    c1 = c + 1 - 2 * lax.rem(c, 2)
    c2 = lax.rem(c + 2, 4)
    own = lax.rem(c, 2)
    other_side, own_side = 1 - c // 2, c // 2

    def place(s, seq, chan):
        return (s, seq, chan)

    rows_copy = pltpu.make_async_copy(rows_hbm, rows_v, local_sem.at[0])
    rows_copy.start()
    table_copy = pltpu.make_async_copy(table_hbm, table, local_sem.at[1])
    table_copy.start()
    n1 = table.shape[0] - 4 * LANES - 3 * k_rows
    forward_ref = table.at[: 2 * LANES]
    back_ref = table.at[2 * LANES : 4 * LANES]
    twist_ref = [
        table.at[4 * LANES : 4 * LANES + k_rows, :LANES],
        table.at[4 * LANES : 4 * LANES + k_rows, LANES:],
    ]
    first_ref = table.at[4 * LANES + k_rows : 4 * LANES + 3 * k_rows, :n1]
    last_ref = table.at[4 * LANES + 3 * k_rows :, : 2 * k_rows]

    barrier = pltpu.get_barrier_semaphore()

    def greet(i, carry):
        pl.semaphore_signal(
            barrier, inc=1, device_id=place(ahead, i // n_chan, i % n_chan), device_id_type=MESH
        )
        return carry

    lax.fori_loop(0, n_seq * n_chan, greet, 0)
    for other in range(n_chan):
        pl.semaphore_signal(barrier, inc=1, device_id=place(behind, z, other), device_id_type=MESH)
    pl.semaphore_signal(barrier, inc=1, device_id=place(sec, z, c1), device_id_type=MESH)
    pl.semaphore_signal(barrier, inc=1, device_id=place(sec, z, c2), device_id_type=MESH)
    for step in range(1, n_seq):
        pl.semaphore_signal(
            barrier, inc=1, device_id=place(sec, lax.rem(z + step, n_seq), c), device_id_type=MESH
        )
    pl.semaphore_wait(barrier, n_seq * n_chan + n_chan + 2 + n_seq - 1)

    def remote(src, dst, send, recv, target):
        return pltpu.make_async_remote_copy(
            src_ref=src, dst_ref=dst, send_sem=send, recv_sem=recv, device_id=target,
            device_id_type=MESH,
        )

    me = z * n_chan + c

    def filter_copy(i):
        seq, chan = i // n_chan, i % n_chan
        return remote(
            filter_hbm.at[chan * n_seq + seq], fil_in.at[me], f_send.at[i], f_recv.at[me],
            place(behind, seq, chan),
        )

    def filter_wait(i):
        return remote(
            filter_hbm.at[0], fil_in.at[i], f_send.at[i], f_recv.at[i], place(behind, z, c)
        )

    def start_filter(i, carry):
        filter_copy(i).start()
        return carry

    def end_filter(i, carry):
        filter_copy(i).wait_send()
        filter_wait(i).wait_recv()
        return carry

    total = BLOCKS * PIECES
    positions, features = rows_v.shape
    depth = features // (2 * PIECES)
    pair = 2 * group

    def block_of(j):
        return (j % 3) * 2 + (other_side if j < 3 else own_side)

    def over_y(k):
        block, at = block_of(k // PIECES), half * PIECES + k % PIECES
        source = weight_hbm.at[
            pl.ds(pl.multiple_of(at * depth, depth), depth),
            pl.ds(pl.multiple_of(block * pair, pair), pair),
        ]
        return remote(
            source, wbuf.at[block, at], y_send.at[k], y_recv.at[k], place(behind, z, c)
        )

    def over_z(k):
        block, at = block_of(k // PIECES), half * PIECES + k % PIECES
        held_piece = wbuf.at[block, at]
        return remote(held_piece, held_piece, z_send.at[k], z_recv.at[k], place(sec, mate, c))

    def from_z(k):
        block, at = block_of(k // PIECES), (1 - half) * PIECES + k % PIECES
        held_piece = wbuf.at[block, at]
        return remote(held_piece, held_piece, z_send.at[k], z_recv.at[k], place(sec, mate, c))

    pos_tile = 512
    own_rows = pl.ds(pl.multiple_of(own * group, group), group)
    pair_rows = pl.ds(pl.multiple_of((1 - own) * group, group), group)

    def multiply(j):
        block = wbuf[block_of(j)].reshape(features, pair)

        def tile(t, carry):
            at = pl.multiple_of(t * pos_tile, pos_tile)
            part[j, :, pl.ds(at, pos_tile)] = jnp.dot(
                rows_v[pl.ds(at, pos_tile), :], block, preferred_element_type=F32
            ).T
            return carry

        lax.fori_loop(0, positions // pos_tile, tile, 0)

    def to_pair(j):
        return remote(
            part.at[j, pair_rows], held.at[j], r_send.at[j], r_recv.at[j], place(sec, z, c1)
        )

    def to_cross(j):
        return remote(
            part.at[j, own_rows], crossed.at[j], r_send.at[BLOCKS + j], r_recv.at[BLOCKS + j],
            place(sec, z, c2),
        )

    def spectrum(target):
        for a in range(share):
            line[:, a * LANES : (a + 1) * LANES] = stack[a]
        mixed = exact(first_ref[...], line[...])
        for a in range(share):
            lanes = slice(a * LANES, (a + 1) * LANES)
            real, imag = mixed[:k_rows, lanes], mixed[k_rows:, lanes]
            span = slice(a * k_rows, (a + 1) * k_rows)
            spec_in[span, :LANES] = real * twist_ref[0][...] + imag * twist_ref[1][...]
            spec_in[span, LANES:] = imag * twist_ref[0][...] - real * twist_ref[1][...]
        target[...] = exact(spec_in[...], forward_ref[...])

    def process(j):
        for k in range(j * PIECES, (j + 1) * PIECES):
            from_z(k).wait_recv()
        multiply(j)
        to_pair(j).start()
        if 1 <= j <= 3:
            to_pair(j - 1).wait_recv()
            part[j - 1, own_rows] = part[j - 1, own_rows] + held[j - 1]
            to_cross(j - 1).start()

    lax.fori_loop(0, n_seq * n_chan, start_filter, 0)
    for k in range(AHEAD):
        over_y(k).start()
    rows_copy.wait()
    table_copy.wait()
    for k in range(total):
        over_y(k).wait_recv()
        over_z(k).start()
        over_y(k).wait_send()
        if k + AHEAD < total:
            over_y(k + AHEAD).start()
        if k % PIECES == PIECES - 1 and k >= PIECES:
            process(k // PIECES - 1)
    process(BLOCKS - 1)
    gathered = []
    for t in range(3):
        to_cross(t).wait_recv()
        to_pair(3 + t).wait_recv()
        total_part = part[3 + t, own_rows] + held[3 + t] + crossed[t]
        gathered.append(total_part.astype(jnp.bfloat16).astype(F32))
    query[...] = gathered[0]
    signal = gathered[1] * gathered[2]
    for i in range(n_seq):
        sig_out[i] = signal[i * share : (i + 1) * share].astype(jnp.bfloat16)

    def sig_copy(step):
        to = lax.rem(z + step, n_seq)
        return remote(
            sig_out.at[to], sig_in.at[z], a_send.at[step], a_recv.at[step],
            place(sec, to, c),
        )

    def sig_wait(step):
        source = lax.rem(z + n_seq - step, n_seq)
        return remote(
            sig_out.at[0], sig_in.at[source], a_send.at[step], a_recv.at[step],
            place(sec, source, c),
        )

    for step in range(1, n_seq):
        sig_copy(step).start()
    sig_in[z] = sig_out[z]
    lax.fori_loop(0, n_seq * n_chan, end_filter, 0)
    per = fil_in.shape[2] // LANES
    for i in range(n_seq * n_chan):
        block = fil_in[i].astype(F32)
        for r in range(per):
            stack[:, i * per + r, :] = block[:, r * LANES : (r + 1) * LANES]
    spectrum(fil_spec)
    for step in range(1, n_seq):
        sig_wait(step).wait_recv()

    for i in range(n_seq):
        block = sig_in[i].astype(F32)
        for r in range(tile_rows):
            stack[:, i * tile_rows + r, :] = block[:, r * LANES : (r + 1) * LANES]
    spectrum(sig_spec)
    spec = sig_spec[...]
    sr, si = spec[:, :LANES], spec[:, LANES:]
    fr, fi = fil_spec[:, :LANES], fil_spec[:, LANES:]
    spec_in[:, :LANES] = sr * fr - si * fi
    spec_in[:, LANES:] = sr * fi + si * fr
    inner = exact(spec_in[...], back_ref[...])
    turned = []
    for a in range(share):
        span = slice(a * k_rows, (a + 1) * k_rows)
        real, imag = inner[span, :LANES], inner[span, LANES:]
        turned.append(
            jnp.concatenate(
                [
                    real * twist_ref[0][...] - imag * twist_ref[1][...],
                    imag * twist_ref[0][...] + real * twist_ref[1][...],
                ],
                axis=0,
            )
        )
    conv = exact(last_ref[...], jnp.concatenate(turned, axis=1))
    for a in range(share):
        stack[a] = conv[:, a * LANES : (a + 1) * LANES]
    for i in range(n_seq):
        for r in range(tile_rows):
            conv_out[i, :, r * LANES : (r + 1) * LANES] = stack[:, i * tile_rows + r, :].astype(
                jnp.bfloat16
            )

    def conv_copy(step):
        to = lax.rem(z + step, n_seq)
        return remote(
            conv_out.at[to], conv_in.at[z], b_send.at[step], b_recv.at[step], place(sec, to, c)
        )

    def conv_wait(step):
        source = lax.rem(z + n_seq - step, n_seq)
        return remote(
            conv_out.at[0], conv_in.at[source], b_send.at[step], b_recv.at[step],
            place(sec, source, c),
        )

    for step in range(1, n_seq):
        conv_copy(step).start()
    conv_in[z] = conv_out[z]
    for step in range(1, n_seq):
        conv_wait(step).wait_recv()

    per = tile_rows // n_chan
    gated = query[...] * conv_in[...].astype(F32).reshape(group, positions)
    for to in range(n_chan):
        gate_out[to] = gated[:, to * per * LANES : (to + 1) * per * LANES].astype(jnp.bfloat16)

    def gate_copy(to):
        return remote(
            gate_out.at[to], gate_in.at[c], o_send.at[to], o_recv.at[c], place(ahead, z, to)
        )

    def gate_wait(source):
        return remote(
            gate_out.at[0], gate_in.at[source], o_send.at[source], o_recv.at[source],
            place(ahead, z, source),
        )

    for to in range(n_chan):
        gate_copy(to).start()
    for source in range(n_chan):
        gate_wait(source).wait_recv()
    whole = gate_in[...].astype(F32).reshape(n_chan * group, per * LANES)
    out_ref[...] = whole.T.astype(jnp.bfloat16)

    for k in range(total):
        over_z(k).wait_send()
    for j in range(BLOCKS):
        to_pair(j).wait_send()
    for j in range(3):
        to_cross(j).wait_send()
    for step in range(1, n_seq):
        sig_copy(step).wait_send()
        conv_copy(step).wait_send()
    for to in range(n_chan):
        gate_copy(to).wait_send()


def body(n_sec, n_seq, n_chan, layer_rows, in_weight, long_filter, skip_gain):
    chan_width = long_filter.shape[2]
    block = long_filter.shape[1]
    positions, features = layer_rows.shape[1:]
    group = chan_width // n_chan
    share = group // n_seq
    tile_rows = positions // LANES
    n1 = n_seq * tile_rows
    table = packed_tables(n_seq * positions)
    k_rows = (table.shape[0] - 4 * LANES - n1) // 3
    weight = in_weight[0]
    pair = 2 * group
    at_start = lax.axis_index(("seq", "chan")) == 0
    tap = jnp.where(at_start, skip_gain[0], 0.0)
    taps = jnp.concatenate([long_filter[0, :1] + tap[None, :], long_filter[0, 1:]], axis=0)
    taps = taps.astype(jnp.bfloat16).T.reshape(n_chan * n_seq, share, block)
    sizes = (n_sec, n_seq, n_chan, group, share, tile_rows, k_rows)
    vmem = pl.BlockSpec(memory_space=pltpu.VMEM)
    hbm = pl.BlockSpec(memory_space=pl.ANY)
    dma = pltpu.SemaphoreType.DMA
    devices = n_seq * n_chan
    total = BLOCKS * PIECES
    scratch = [
        pltpu.VMEM(table.shape, F32),
        pltpu.VMEM((positions, features), jnp.bfloat16),
        pltpu.VMEM((BLOCKS, 2 * PIECES, features // (2 * PIECES), pair), jnp.bfloat16),
        pltpu.VMEM((BLOCKS, pair, positions), F32),
        pltpu.VMEM((BLOCKS, group, positions), F32),
        pltpu.VMEM((3, group, positions), F32),
        pltpu.VMEM((devices, share, block), jnp.bfloat16),
        pltpu.VMEM((n_seq, share, positions), jnp.bfloat16),
        pltpu.VMEM((n_seq, share, positions), jnp.bfloat16),
        pltpu.VMEM((group, positions), F32),
        pltpu.VMEM((n_seq, share, positions), jnp.bfloat16),
        pltpu.VMEM((n_seq, share, positions), jnp.bfloat16),
        pltpu.VMEM((n_chan, group, block), jnp.bfloat16),
        pltpu.VMEM((n_chan, group, block), jnp.bfloat16),
        pltpu.VMEM((share, n1, LANES), F32),
        pltpu.VMEM((n1, share * LANES), F32),
        pltpu.VMEM((share * k_rows, 2 * LANES), F32),
        pltpu.VMEM((share * k_rows, 2 * LANES), F32),
        pltpu.VMEM((share * k_rows, 2 * LANES), F32),
        dma((total,)), dma((total,)), dma((total,)), dma((total,)), dma((BLOCKS + 3,)),
        dma((BLOCKS + 3,)),
        dma((devices,)), dma((devices,)), dma((n_seq,)), dma((n_seq,)), dma((n_seq,)),
        dma((n_seq,)), dma((n_chan,)), dma((n_chan,)), dma((2,)),
    ]
    out = pl.pallas_call(
        functools.partial(kernel, sizes),
        out_shape=jax.ShapeDtypeStruct((block, chan_width), jnp.bfloat16),
        in_specs=[hbm, hbm, hbm, hbm],
        out_specs=vmem,
        scratch_shapes=scratch,
        compiler_params=pltpu.CompilerParams(
            collective_id=0, has_side_effects=True, vmem_limit_bytes=60 * 2**20
        ),
        cost_estimate=pl.CostEstimate(
            flops=2 * positions * features * 3 * chan_width,
            bytes_accessed=10 * 2**20, transcendentals=0,
        ),
    )(layer_rows[0], weight, taps, table)
    return out[None]


def solution(mesh):
    in_specs = (
        P("section", "seq", "chan"),
        P("section", "chan", None),
        P("section", ("seq", "chan"), None),
        P("section", None),
    )
    out_specs = P("section", ("seq", "chan"), None)
    call = functools.partial(
        body, mesh.shape["section"], mesh.shape["seq"], mesh.shape["chan"]
    )
    return jax.shard_map(call, mesh=mesh, in_specs=in_specs, out_specs=out_specs, check_vma=False)
```

```python
import functools
import math

import jax
import jax.numpy as jnp
import numpy as np
from jax import lax
from jax.experimental import pallas as pl
from jax.experimental.pallas import tpu as pltpu
from jax.sharding import PartitionSpec as P

LANES = 128
PIECES = 2
BLOCKS = 6
AHEAD = 2
MESH = pl.DeviceIdType.MESH
F32 = jnp.float32


def tables(positions):
    length = 2 * positions
    n1 = positions // LANES
    full = 2 * n1
    kept = n1 + 1
    rows = -(-kept // 8) * 8
    k1 = np.arange(kept)
    angle = 2 * math.pi * ((k1[:, None] * np.arange(n1)[None, :]) % full) / full
    first = np.zeros((2 * rows, n1), np.float32)
    first[:kept] = np.cos(angle)
    first[rows : rows + kept] = -np.sin(angle)
    weight = np.where((k1 == 0) | (k1 == n1), 1.0, 2.0) / length
    last = np.zeros((n1, 2 * rows), np.float32)
    last[:, :kept] = (np.cos(angle) * weight[:, None]).T
    last[:, rows : rows + kept] = -(np.sin(angle) * weight[:, None]).T
    n2 = np.arange(LANES)
    turn = 2 * math.pi * ((np.arange(rows)[:, None] * n2[None, :]) % length) / length
    twist = np.stack([np.cos(turn), np.sin(turn)]).astype(np.float32)
    fine = 2 * math.pi * ((n2[:, None] * n2[None, :]) % LANES) / LANES
    cos, sin = np.cos(fine), np.sin(fine)
    forward = np.block([[cos, -sin], [sin, cos]]).astype(np.float32)
    back = np.block([[cos, sin], [-sin, cos]]).astype(np.float32)
    return first, twist, forward, back, last


def packed_tables(positions):
    first, twist, forward, back, last = tables(positions)
    wide = [forward, back, np.concatenate([twist[0], twist[1]], axis=1), first, last]
    return np.concatenate([np.pad(t, ((0, 0), (0, 2 * LANES - t.shape[1]))) for t in wide])


def parts_of(a):
    high = a.astype(jnp.bfloat16)
    return high, (a - high.astype(F32)).astype(jnp.bfloat16)


def exact(a, b):
    a_high, a_low = parts_of(a)
    b_high, b_low = parts_of(b)
    dot = functools.partial(jnp.dot, preferred_element_type=F32)
    return dot(a_high, b_high) + (dot(a_high, b_low) + dot(a_low, b_high))


def kernel(
    sizes,
    rows_hbm, weight_hbm, filter_hbm, table_hbm,
    out_ref,
    table, rows_v, wbuf, part, held, crossed, fil_in, sig_out, sig_in, query, conv_out, conv_in, gate_out, gate_in,
    stack, line, spec_in, fil_spec, sig_spec,
    y_send, y_recv, z_send, z_recv, r_send, r_recv, f_send, f_recv,
    a_send, a_recv, b_send, b_recv, o_send, o_recv, local_sem,
):
    n_sec, n_seq, n_chan, group, share, tile_rows, k_rows = sizes
    sec, z, c = lax.axis_index("section"), lax.axis_index("seq"), lax.axis_index("chan")
    ahead = lax.rem(sec + 1, n_sec)
    behind = lax.rem(sec + n_sec - 1, n_sec)
    half = lax.rem(z, 2)
    mate = z + 1 - 2 * half
    c1 = c + 1 - 2 * lax.rem(c, 2)
    c2 = lax.rem(c + 2, 4)
    own = lax.rem(c, 2)
    other_side, own_side = 1 - c // 2, c // 2

    def place(s, seq, chan):
        return (s, seq, chan)

    rows_copy = pltpu.make_async_copy(rows_hbm, rows_v, local_sem.at[0])
    rows_copy.start()
    table_copy = pltpu.make_async_copy(table_hbm, table, local_sem.at[1])
    table_copy.start()
    n1 = table.shape[0] - 4 * LANES - 3 * k_rows
    forward_ref = table.at[: 2 * LANES]
    back_ref = table.at[2 * LANES : 4 * LANES]
    twist_ref = [
        table.at[4 * LANES : 4 * LANES + k_rows, :LANES],
        table.at[4 * LANES : 4 * LANES + k_rows, LANES:],
    ]
    first_ref = table.at[4 * LANES + k_rows : 4 * LANES + 3 * k_rows, :n1]
    last_ref = table.at[4 * LANES + 3 * k_rows :, : 2 * k_rows]

    barrier = pltpu.get_barrier_semaphore()

    def greet(i, carry):
        pl.semaphore_signal(
            barrier, inc=1, device_id=place(ahead, i // n_chan, i % n_chan), device_id_type=MESH
        )
        return carry

    lax.fori_loop(0, n_seq * n_chan, greet, 0)
    for other in range(n_chan):
        pl.semaphore_signal(barrier, inc=1, device_id=place(behind, z, other), device_id_type=MESH)
    pl.semaphore_signal(barrier, inc=1, device_id=place(sec, z, c1), device_id_type=MESH)
    pl.semaphore_signal(barrier, inc=1, device_id=place(sec, z, c2), device_id_type=MESH)
    for step in range(1, n_seq):
        pl.semaphore_signal(
            barrier, inc=1, device_id=place(sec, lax.rem(z + step, n_seq), c), device_id_type=MESH
        )
    pl.semaphore_wait(barrier, n_seq * n_chan + n_chan + 2 + n_seq - 1)

    def remote(src, dst, send, recv, target):
        return pltpu.make_async_remote_copy(
            src_ref=src, dst_ref=dst, send_sem=send, recv_sem=recv, device_id=target,
            device_id_type=MESH,
        )

    me = z * n_chan + c

    def filter_copy(i):
        seq, chan = i // n_chan, i % n_chan
        return remote(
            filter_hbm.at[chan * n_seq + seq], fil_in.at[me], f_send.at[i], f_recv.at[me],
            place(behind, seq, chan),
        )

    def filter_wait(i):
        return remote(
            filter_hbm.at[0], fil_in.at[i], f_send.at[i], f_recv.at[i], place(behind, z, c)
        )

    def start_filter(i, carry):
        filter_copy(i).start()
        return carry

    def end_filter(i, carry):
        filter_copy(i).wait_send()
        filter_wait(i).wait_recv()
        return carry

    total = BLOCKS * PIECES
    positions, features = rows_v.shape
    depth = features // (2 * PIECES)
    pair = 2 * group

    def block_of(j):
        return (j % 3) * 2 + (other_side if j < 3 else own_side)

    def over_y(k):
        block, at = block_of(k // PIECES), half * PIECES + k % PIECES
        source = weight_hbm.at[
            pl.ds(pl.multiple_of(at * depth, depth), depth),
            pl.ds(pl.multiple_of(block * pair, pair), pair),
        ]
        return remote(
            source, wbuf.at[block, at], y_send.at[k], y_recv.at[k], place(behind, z, c)
        )

    def over_z(k):
        block, at = block_of(k // PIECES), half * PIECES + k % PIECES
        held_piece = wbuf.at[block, at]
        return remote(held_piece, held_piece, z_send.at[k], z_recv.at[k], place(sec, mate, c))

    def from_z(k):
        block, at = block_of(k // PIECES), (1 - half) * PIECES + k % PIECES
        held_piece = wbuf.at[block, at]
        return remote(held_piece, held_piece, z_send.at[k], z_recv.at[k], place(sec, mate, c))

    pos_tile = 512
    own_rows = pl.ds(pl.multiple_of(own * group, group), group)
    pair_rows = pl.ds(pl.multiple_of((1 - own) * group, group), group)

    def multiply(j):
        block = wbuf[block_of(j)].reshape(features, pair)

        def tile(t, carry):
            at = pl.multiple_of(t * pos_tile, pos_tile)
            part[j, :, pl.ds(at, pos_tile)] = jnp.dot(
                rows_v[pl.ds(at, pos_tile), :], block, preferred_element_type=F32
            ).T
            return carry

        lax.fori_loop(0, positions // pos_tile, tile, 0)

    def to_pair(j):
        return remote(
            part.at[j, pair_rows], held.at[j], r_send.at[j], r_recv.at[j], place(sec, z, c1)
        )

    def to_cross(j):
        return remote(
            part.at[j, own_rows], crossed.at[j], r_send.at[BLOCKS + j], r_recv.at[BLOCKS + j],
            place(sec, z, c2),
        )

    def spectrum(target):
        for a in range(share):
            line[:, a * LANES : (a + 1) * LANES] = stack[a]
        mixed = exact(first_ref[...], line[...])
        for a in range(share):
            lanes = slice(a * LANES, (a + 1) * LANES)
            real, imag = mixed[:k_rows, lanes], mixed[k_rows:, lanes]
            span = slice(a * k_rows, (a + 1) * k_rows)
            spec_in[span, :LANES] = real * twist_ref[0][...] + imag * twist_ref[1][...]
            spec_in[span, LANES:] = imag * twist_ref[0][...] - real * twist_ref[1][...]
        target[...] = exact(spec_in[...], forward_ref[...])

    def process(j):
        for k in range(j * PIECES, (j + 1) * PIECES):
            from_z(k).wait_recv()
        multiply(j)
        to_pair(j).start()
        if 1 <= j <= 3:
            to_pair(j - 1).wait_recv()
            part[j - 1, own_rows] = part[j - 1, own_rows] + held[j - 1]
            to_cross(j - 1).start()

    for k in range(AHEAD):
        over_y(k).start()
    rows_copy.wait()
    table_copy.wait()
    for k in range(total):
        over_y(k).wait_recv()
        over_z(k).start()
        over_y(k).wait_send()
        if k + AHEAD < total:
            over_y(k + AHEAD).start()
        if k == total - AHEAD - 2:
            lax.fori_loop(0, n_seq * n_chan, start_filter, 0)
        if k % PIECES == PIECES - 1 and k >= PIECES:
            process(k // PIECES - 1)
    process(BLOCKS - 1)
    gathered = []
    for t in range(3):
        to_cross(t).wait_recv()
        to_pair(3 + t).wait_recv()
        total_part = part[3 + t, own_rows] + held[3 + t] + crossed[t]
        gathered.append(total_part.astype(jnp.bfloat16).astype(F32))
    query[...] = gathered[0]
    signal = gathered[1] * gathered[2]
    for i in range(n_seq):
        sig_out[i] = signal[i * share : (i + 1) * share].astype(jnp.bfloat16)

    def sig_copy(step):
        to = lax.rem(z + step, n_seq)
        return remote(
            sig_out.at[to], sig_in.at[z], a_send.at[step], a_recv.at[step],
            place(sec, to, c),
        )

    def sig_wait(step):
        source = lax.rem(z + n_seq - step, n_seq)
        return remote(
            sig_out.at[0], sig_in.at[source], a_send.at[step], a_recv.at[step],
            place(sec, source, c),
        )

    for step in range(1, n_seq):
        sig_copy(step).start()
    sig_in[z] = sig_out[z]
    lax.fori_loop(0, n_seq * n_chan, end_filter, 0)
    per = fil_in.shape[2] // LANES
    for i in range(n_seq * n_chan):
        block = fil_in[i].astype(F32)
        for r in range(per):
            stack[:, i * per + r, :] = block[:, r * LANES : (r + 1) * LANES]
    spectrum(fil_spec)
    for step in range(1, n_seq):
        sig_wait(step).wait_recv()

    for i in range(n_seq):
        block = sig_in[i].astype(F32)
        for r in range(tile_rows):
            stack[:, i * tile_rows + r, :] = block[:, r * LANES : (r + 1) * LANES]
    spectrum(sig_spec)
    spec = sig_spec[...]
    sr, si = spec[:, :LANES], spec[:, LANES:]
    fr, fi = fil_spec[:, :LANES], fil_spec[:, LANES:]
    spec_in[:, :LANES] = sr * fr - si * fi
    spec_in[:, LANES:] = sr * fi + si * fr
    inner = exact(spec_in[...], back_ref[...])
    turned = []
    for a in range(share):
        span = slice(a * k_rows, (a + 1) * k_rows)
        real, imag = inner[span, :LANES], inner[span, LANES:]
        turned.append(
            jnp.concatenate(
                [
                    real * twist_ref[0][...] - imag * twist_ref[1][...],
                    imag * twist_ref[0][...] + real * twist_ref[1][...],
                ],
                axis=0,
            )
        )
    conv = exact(last_ref[...], jnp.concatenate(turned, axis=1))
    for a in range(share):
        stack[a] = conv[:, a * LANES : (a + 1) * LANES]
    for i in range(n_seq):
        for r in range(tile_rows):
            conv_out[i, :, r * LANES : (r + 1) * LANES] = stack[:, i * tile_rows + r, :].astype(
                jnp.bfloat16
            )

    def conv_copy(step):
        to = lax.rem(z + step, n_seq)
        return remote(
            conv_out.at[to], conv_in.at[z], b_send.at[step], b_recv.at[step], place(sec, to, c)
        )

    def conv_wait(step):
        source = lax.rem(z + n_seq - step, n_seq)
        return remote(
            conv_out.at[0], conv_in.at[source], b_send.at[step], b_recv.at[step],
            place(sec, source, c),
        )

    for step in range(1, n_seq):
        conv_copy(step).start()
    conv_in[z] = conv_out[z]
    for step in range(1, n_seq):
        conv_wait(step).wait_recv()

    per = tile_rows // n_chan
    gated = query[...] * conv_in[...].astype(F32).reshape(group, positions)
    for to in range(n_chan):
        gate_out[to] = gated[:, to * per * LANES : (to + 1) * per * LANES].astype(jnp.bfloat16)

    def gate_copy(to):
        return remote(
            gate_out.at[to], gate_in.at[c], o_send.at[to], o_recv.at[c], place(ahead, z, to)
        )

    def gate_wait(source):
        return remote(
            gate_out.at[0], gate_in.at[source], o_send.at[source], o_recv.at[source],
            place(ahead, z, source),
        )

    for to in range(n_chan):
        gate_copy(to).start()
    for source in range(n_chan):
        gate_wait(source).wait_recv()
    whole = gate_in[...].astype(F32).reshape(n_chan * group, per * LANES)
    out_ref[...] = whole.T.astype(jnp.bfloat16)

    for k in range(total):
        over_z(k).wait_send()
    for j in range(BLOCKS):
        to_pair(j).wait_send()
    for j in range(3):
        to_cross(j).wait_send()
    for step in range(1, n_seq):
        sig_copy(step).wait_send()
        conv_copy(step).wait_send()
    for to in range(n_chan):
        gate_copy(to).wait_send()


def body(n_sec, n_seq, n_chan, layer_rows, in_weight, long_filter, skip_gain):
    chan_width = long_filter.shape[2]
    block = long_filter.shape[1]
    positions, features = layer_rows.shape[1:]
    group = chan_width // n_chan
    share = group // n_seq
    tile_rows = positions // LANES
    n1 = n_seq * tile_rows
    table = packed_tables(n_seq * positions)
    k_rows = (table.shape[0] - 4 * LANES - n1) // 3
    weight = in_weight[0]
    pair = 2 * group
    at_start = lax.axis_index(("seq", "chan")) == 0
    tap = jnp.where(at_start, skip_gain[0], 0.0)
    taps = jnp.concatenate([long_filter[0, :1] + tap[None, :], long_filter[0, 1:]], axis=0)
    taps = taps.astype(jnp.bfloat16).T.reshape(n_chan * n_seq, share, block)
    sizes = (n_sec, n_seq, n_chan, group, share, tile_rows, k_rows)
    vmem = pl.BlockSpec(memory_space=pltpu.VMEM)
    hbm = pl.BlockSpec(memory_space=pl.ANY)
    dma = pltpu.SemaphoreType.DMA
    devices = n_seq * n_chan
    total = BLOCKS * PIECES
    scratch = [
        pltpu.VMEM(table.shape, F32),
        pltpu.VMEM((positions, features), jnp.bfloat16),
        pltpu.VMEM((BLOCKS, 2 * PIECES, features // (2 * PIECES), pair), jnp.bfloat16),
        pltpu.VMEM((BLOCKS, pair, positions), F32),
        pltpu.VMEM((BLOCKS, group, positions), F32),
        pltpu.VMEM((3, group, positions), F32),
        pltpu.VMEM((devices, share, block), jnp.bfloat16),
        pltpu.VMEM((n_seq, share, positions), jnp.bfloat16),
        pltpu.VMEM((n_seq, share, positions), jnp.bfloat16),
        pltpu.VMEM((group, positions), F32),
        pltpu.VMEM((n_seq, share, positions), jnp.bfloat16),
        pltpu.VMEM((n_seq, share, positions), jnp.bfloat16),
        pltpu.VMEM((n_chan, group, block), jnp.bfloat16),
        pltpu.VMEM((n_chan, group, block), jnp.bfloat16),
        pltpu.VMEM((share, n1, LANES), F32),
        pltpu.VMEM((n1, share * LANES), F32),
        pltpu.VMEM((share * k_rows, 2 * LANES), F32),
        pltpu.VMEM((share * k_rows, 2 * LANES), F32),
        pltpu.VMEM((share * k_rows, 2 * LANES), F32),
        dma((total,)), dma((total,)), dma((total,)), dma((total,)), dma((BLOCKS + 3,)),
        dma((BLOCKS + 3,)),
        dma((devices,)), dma((devices,)), dma((n_seq,)), dma((n_seq,)), dma((n_seq,)),
        dma((n_seq,)), dma((n_chan,)), dma((n_chan,)), dma((2,)),
    ]
    out = pl.pallas_call(
        functools.partial(kernel, sizes),
        out_shape=jax.ShapeDtypeStruct((block, chan_width), jnp.bfloat16),
        in_specs=[hbm, hbm, hbm, hbm],
        out_specs=vmem,
        scratch_shapes=scratch,
        compiler_params=pltpu.CompilerParams(
            collective_id=0, has_side_effects=True, vmem_limit_bytes=60 * 2**20
        ),
        cost_estimate=pl.CostEstimate(
            flops=2 * positions * features * 3 * chan_width,
            bytes_accessed=10 * 2**20, transcendentals=0,
        ),
    )(layer_rows[0], weight, taps, table)
    return out[None]


def solution(mesh):
    in_specs = (
        P("section", "seq", "chan"),
        P("section", "chan", None),
        P("section", ("seq", "chan"), None),
        P("section", None),
    )
    out_specs = P("section", ("seq", "chan"), None)
    call = functools.partial(
        body, mesh.shape["section"], mesh.shape["seq"], mesh.shape["chan"]
    )
    return jax.shard_map(call, mesh=mesh, in_specs=in_specs, out_specs=out_specs, check_vma=False)
```
